256 devices in a mesh: dp: 8 (over x, core), expert: 32 (over z, y).
Axes of the slice: x: 4, y: 4, z: 8, core: 2. Of those that a mesh axis runs over, the one named last changes fastest.
Arguments:
- tokens: bfloat16 [32768, 8192], P(('dp', 'expert')), may hold values from -6 to 6
- cotangent: bfloat16 [32768, 8192], P(('dp', 'expert')), may hold values from -0.125 to 0.125
- routes: int32 [32768, 2], P(('dp', 'expert')), may hold values from 0 to 31, all different within a row; in each aligned block of 128 rows (0 to 127, 128 to 255, ...) at most 9 rows name the same one
- combine_weights: float32 [32768, 2], P(('dp', 'expert')), may hold values from 0.2 to 1
- gate_dense: bfloat16 [8192, 14336], P(('dp', 'expert')), may hold values from -0.0625 to 0.0625
- up_dense: bfloat16 [8192, 14336], P(('dp', 'expert')), may hold values from -0.0625 to 0.0625
- down_dense: bfloat16 [8192, 14336], P(('dp', 'expert')), may hold values from -0.25 to 0.25
Outputs:
- grad_gate: float32 [8192, 14336], P('dp', 'expert')
- grad_up: float32 [8192, 14336], P('dp', 'expert')
- grad_down: float32 [8192, 14336], P('dp', 'expert')
The draws below stay inside these ranges and needn't reach their ends.
Inputs may be any that keep to these rules, and one draw needn't show every extreme that they name: `routes`: the 2 experts of a token differ. Among the tokens of one device no expert is chosen more than 9 times, and in some device one expert is chosen exactly 9 times.
All inputs are finite; a program needn't handle non-finite values.
Results may differ from the reference program's by a relative error of at most 0.004.
Values may be sent and summed in bfloat16 or wider, within the bound.
No kernel may reach another device: no remote copies, remote signals or barrier semaphores. Data moves between devices by JAX's collectives and lax.ppermute only.
A program may use at most 192 MiB of HBM per device.

```python
import math
import jax
import jax.numpy as jnp
import numpy as np
from jax import lax

D = 8192
HID = 448
TOP = 2
TOK_DEV = 128
EXPERTS = 32
FFW = 14336
CAP = 9
TOKENS = 32768
DEVICES = 256


def steps_of(own_key, extent, shards, low, top_value):
    def one(dim, parts):
        heights = jax.random.uniform(jax.random.fold_in(jax.random.fold_in(own_key, 6), dim), (parts,), jnp.float32, low / len(shards), top_value / len(shards))
        return jnp.repeat(jnp.exp(heights), extent[dim] // parts).reshape((-1,) + (1,) * (len(extent) - dim - 1))

    loudness = one(*shards[0])
    for cut in shards[1:]:
        loudness = loudness * one(*cut)
    return loudness


def shared_out(rng, own, number, rows, count, top, most, skew):
    sequence = jax.random.permutation(rng, count)
    crowded, usual = shares(count, rows * top, most, skew, True), shares(count, rows * top, most, skew, False)
    places = jnp.arange(count)

    def named(sizes, turn):
        used = int((sizes > 0).sum())
        fixed = max(1, used // 4)
        passed = fixed + (places - fixed + turn * (used - fixed)) % max(1, count - fixed)
        return jnp.zeros((count,), jnp.int32).at[sequence[jnp.where(places < fixed, places, passed)]].set(jnp.asarray(sizes, jnp.int32))

    sizes = jnp.where(number % 4 == 0, named(crowded, number // 4), named(usual, number - number // 4 - 1))
    mixed = jax.random.permutation(jax.random.fold_in(own, 3), count)
    giver, taker = mixed[0:count // 2 * 2:2], mixed[1:count // 2 * 2:2]
    slack = jnp.minimum(sizes[giver] - 1, most - sizes[taker]) // 2
    slack = jnp.where((giver == sequence[0]) | (taker == sequence[0]) | (sizes[taker] == 0), 0, jnp.maximum(slack, 0))
    passed = jax.random.randint(jax.random.fold_in(own, 4), (count // 2,), 0, 1 << 20) % (slack + 1)
    sizes = sizes.at[giver].add(-passed).at[taker].add(passed)
    items = jnp.searchsorted(jnp.cumsum(sizes), jnp.arange(rows * top), side="right").astype(jnp.int32)
    table = items.reshape(top, rows).T
    table = table[jax.random.permutation(jax.random.fold_in(own, 1), rows)]
    turn = jax.random.randint(jax.random.fold_in(own, 2), (rows, 1), 0, top)
    return jnp.take_along_axis(table, (jnp.arange(top)[None, :] + turn) % top, axis=1)


def shares(count, total, limit, skew, full):
    loads = [(1 << 20) // math.isqrt(grade ** skew) + 1 for grade in range(1, count + 1)]
    largest = limit if full else min(limit, max(-(-total // count), total * loads[0] // sum(loads)))
    least = 1 if total - largest >= count - 1 else 0
    given, spare = [largest] + [least] * (count - 1), total - largest - least * (count - 1)
    while spare > 0:
        candidates = [i for i in range(1, count) if given[i] < largest] or [i for i in range(1, count) if given[i] < limit]
        mass, left = sum([loads[i] for i in candidates]), spare
        for i in candidates:
            extra = min(limit - given[i], max(1, left * loads[i] // mass), spare)
            given[i] = given[i] + extra
            spare = spare - extra
    return np.array(given)


def centred(stream_key, extent, deviation, most, cuts=(), kind=jnp.bfloat16):
    result = jax.random.normal(stream_key, extent, jnp.float32) * deviation
    if len(cuts) > 0:
        result = steps_of(stream_key, extent, cuts, -0.22, 0.18) * result
    return jnp.clip(result, min=-most, max=most).astype(kind)


def setup_inputs(seed: int = 0) -> dict:
    keys = jax.random.split(jax.random.key(seed), 8)
    tokens = centred(keys[0], (TOKENS, D), 1.0, 6.0, ((0, 256),))
    cotangent = centred(keys[1], (TOKENS, D), 0.02, 0.125, ((0, 256),))
    routes_keys = jax.random.split(jax.random.fold_in(keys[2], 1), TOKENS // TOK_DEV)
    routes_turns = jax.random.permutation(jax.random.fold_in(keys[2], 3), TOKENS // TOK_DEV)
    routes = jax.vmap(lambda own, number: shared_out(jax.random.fold_in(keys[2], 2), own, number, TOK_DEV, EXPERTS, TOP, CAP, 1))(routes_keys, routes_turns).reshape((TOKENS, TOP))
    combine_weights = jnp.clip(jnp.exp(math.log(1.0) - 1.609438 * jax.random.uniform(keys[3], (TOKENS, TOP), jnp.float32) ** steps_of(keys[3], (TOKENS, TOP), ((0, 256),), -0.2, 0.2)), 0.2, 1.0)
    gate_dense = centred(keys[4], (D, FFW), D ** -0.5, 0.0625, ((0, 256),))
    up_dense = centred(keys[5], (D, FFW), D ** -0.5, 0.0625, ((0, 256),))
    down_dense = centred(keys[6], (D, FFW), HID ** -0.5, 0.25, ((0, 256),))
    return dict(tokens=tokens, cotangent=cotangent, routes=routes, combine_weights=combine_weights, gate_dense=gate_dense, up_dense=up_dense, down_dense=down_dense)


def silu_parts(gate_vals):
    sigma = jax.nn.sigmoid(gate_vals)
    return gate_vals * sigma, sigma * (1.0 + gate_vals * (1.0 - sigma))


def reference(tokens, cotangent, routes, combine_weights, gate_dense, up_dense, down_dense):
    amount = TOKENS * TOP
    slots_all = DEVICES * CAP
    flat_routes = routes.reshape(DEVICES, TOK_DEV * TOP)
    one_hot = (flat_routes[:, :, None] == jnp.arange(EXPERTS, dtype=jnp.int32)[None, None, :]).astype(jnp.int32)
    rank_in = jnp.cumsum(one_hot, axis=1, dtype=jnp.int32) - 1
    slot_pos = jnp.sum(one_hot * rank_in, axis=2, dtype=jnp.int32)
    source_ids = jnp.arange(DEVICES, dtype=jnp.int32)[:, None]
    position = (source_ids * CAP + slot_pos).reshape(amount)
    owner_id = flat_routes.reshape(amount)
    scaled = (combine_weights[:, :, None] * cotangent[:, None, :].astype(jnp.float32)).astype(jnp.bfloat16)
    scaled = scaled.reshape(amount, D)
    numbers = jnp.arange(amount, dtype=jnp.int32)

    def one_expert(expert_id):
        target = jnp.where(owner_id == expert_id, position, slots_all).astype(jnp.int32)
        row_index = jnp.full((slots_all,), amount, jnp.int32).at[target].set(numbers, mode="drop")
        valid = (row_index < amount).astype(jnp.bfloat16)[:, None]
        safe = jnp.minimum(row_index, amount - 1).astype(jnp.int32)
        rows_x = jnp.take(tokens, safe // TOP, axis=0) * valid
        rows_dy = jnp.take(scaled, safe, axis=0) * valid
        start = (expert_id * HID).astype(jnp.int32)
        w_gate = lax.dynamic_slice_in_dim(gate_dense, start, HID, 1)
        w_up = lax.dynamic_slice_in_dim(up_dense, start, HID, 1)
        w_down = lax.dynamic_slice_in_dim(down_dense, start, HID, 1)
        gate_vals = jnp.dot(rows_x, w_gate, preferred_element_type=jnp.float32)
        up_vals = jnp.dot(rows_x, w_up, preferred_element_type=jnp.float32)
        active, slope = silu_parts(gate_vals)
        hidden = (active * up_vals).astype(jnp.bfloat16)
        back = jnp.dot(rows_dy, w_down, preferred_element_type=jnp.float32)
        d_gate = (back * up_vals * slope).astype(jnp.bfloat16)
        d_up = (back * active).astype(jnp.bfloat16)
        g_gate = jnp.dot(rows_x.T, d_gate, preferred_element_type=jnp.float32)
        g_up = jnp.dot(rows_x.T, d_up, preferred_element_type=jnp.float32)
        g_down = jnp.dot(rows_dy.T, hidden, preferred_element_type=jnp.float32)
        return g_gate, g_up, g_down

    stacked = lax.map(one_expert, jnp.arange(EXPERTS, dtype=jnp.int32))
    results = [jnp.transpose(piece, (1, 0, 2)).reshape(D, FFW) for piece in stacked]
    return (results[0], results[1], results[2])
```

```python
import jax
import jax.numpy as jnp
from jax import lax
from jax.experimental import pallas as pl
from jax.experimental.pallas import tpu as pltpu
from jax.sharding import Mesh, PartitionSpec as P

F32 = jnp.float32
BF16 = jnp.bfloat16
VMEM_LIMIT = 48 * 1024 * 1024


def iota(shape, dim):
    return lax.broadcasted_iota(jnp.int32, shape, dim)


def one_if(mask):
    return jnp.where(mask, 1.0, 0.0).astype(BF16)


def pack_rows(routes_t, weights_t, source, owners, blocks, scale):
    rows, width = source.shape
    part = width // blocks
    tiles = part // 128
    main = owners * 8

    def kernel(routes_ref, weights_ref, source_ref, out_ref, pick_ref, factor_ref):
        @pl.when(pl.program_id(0) == 0)
        def _():
            row = iota((2 * main, rows), 0)
            expert = lax.shift_right_logical(jnp.where(row < main, row, row - main), 3)
            first = routes_ref[0:1, :] == expert
            second = routes_ref[1:2, :] == expert
            named = first | second
            before = one_if(iota((rows, rows), 0) < iota((rows, rows), 1))
            rank = jnp.dot(one_if(named), before, preferred_element_type=F32)
            wanted = jnp.where(row < main, jnp.bitwise_and(row, 7), 8).astype(F32)
            picked = named & (rank == wanted)
            pick_ref[...] = one_if(picked)
            value = jnp.where(first, weights_ref[0:1, :], 0.0) + jnp.where(
                second, weights_ref[1:2, :], 0.0
            )
            factor_ref[...] = jnp.sum(jnp.where(picked, value, 0.0), axis=1, keepdims=True)

        val = jnp.dot(pick_ref[...], source_ref[...], preferred_element_type=F32)
        if scale:
            val = val * factor_ref[...]
        sub = jnp.bitwise_and(iota((main, 128), 0), 7)
        ninth = jnp.zeros((main, 128), F32)
        for j in range(tiles):
            cols = slice(128 * j, 128 * (j + 1))
            out_ref[0, :, 8 * j : 8 * (j + 1), :] = (
                val[:main, cols].reshape(owners, 8, 128).astype(BF16)
            )
            ninth = jnp.where(sub == j, val[main:, cols], ninth)
        out_ref[0, :, 8 * tiles :, :] = ninth.reshape(owners, 8, 128).astype(BF16)

    return pl.pallas_call(
        kernel,
        grid=(blocks,),
        in_specs=[
            pl.BlockSpec((2, rows), lambda i: (0, 0)),
            pl.BlockSpec((2, rows), lambda i: (0, 0)),
            pl.BlockSpec((rows, part), lambda i: (0, i)),
        ],
        out_specs=pl.BlockSpec((1, owners, 9 * tiles, 128), lambda i: (i, 0, 0, 0)),
        out_shape=jax.ShapeDtypeStruct((blocks, owners, 9 * tiles, 128), BF16),
        scratch_shapes=[pltpu.VMEM((2 * main, rows), BF16), pltpu.VMEM((2 * main, 1), F32)],
        compiler_params=pltpu.CompilerParams(vmem_limit_bytes=VMEM_LIMIT),
        cost_estimate=pl.CostEstimate(
            flops=4 * main * rows * width, bytes_accessed=2 * width * (rows + 9 * owners), transcendentals=0
        ),
        name="pack_rows",
    )(routes_t, weights_t, source)


def pack_weights(gate, up, down, owners):
    depth, total = gate.shape
    pair = 2 * total // owners
    wide = 512

    def kernel(gate_ref, up_ref, down_ref, out_ref):
        for n, ref in enumerate((gate_ref, up_ref, down_ref)):
            out_ref[0, :, n * wide : (n + 1) * wide] = ref[:, :wide]
            out_ref[1, :, n * wide : (n + 1) * wide] = ref[:, pair - wide :]

    spec = pl.BlockSpec((depth, pair), lambda i: (0, i))
    return pl.pallas_call(
        kernel,
        grid=(owners // 2,),
        in_specs=[spec, spec, spec],
        out_specs=pl.BlockSpec((2, depth, 3 * wide), lambda i: (i, 0, 0)),
        out_shape=jax.ShapeDtypeStruct((owners, depth, 3 * wide), BF16),
        cost_estimate=pl.CostEstimate(
            flops=0, bytes_accessed=2 * depth * (3 * total + owners * 3 * wide), transcendentals=0
        ),
        name="pack_weights",
    )(gate, up, down)


def unpack_and_multiply(received, weight, group):
    senders, height, _ = received.shape
    tiles = height // 9
    depth, columns = weight.shape
    main = group * 8
    rows = group * 9
    steps = senders // group

    def kernel(received_ref, weight_ref, rows_ref, product_ref):
        for j in range(tiles):
            rows_ref[:main, 128 * j : 128 * (j + 1)] = (
                received_ref[:, 8 * j : 8 * (j + 1), :].astype(F32).reshape(main, 128).astype(BF16)
            )
        last = received_ref[:, 8 * tiles :, :].astype(F32).reshape(main, 128).astype(BF16)
        row, col = iota((main, main), 0), iota((main, main), 1)
        turn = one_if(
            (row % group == lax.shift_right_logical(col, 3)) & (row // group == jnp.bitwise_and(col, 7))
        )
        ninth = jnp.dot(turn, last, preferred_element_type=F32).astype(BF16)
        for j in range(tiles):
            rows_ref[main:, 128 * j : 128 * (j + 1)] = ninth[group * j : group * (j + 1)]
        product_ref[...] = jnp.dot(rows_ref[...], weight_ref[...], preferred_element_type=F32)

    return pl.pallas_call(
        kernel,
        grid=(steps,),
        in_specs=[
            pl.BlockSpec((group, height, 128), lambda i: (i, 0, 0)),
            pl.BlockSpec((depth, columns), lambda i: (0, 0)),
        ],
        out_specs=[
            pl.BlockSpec((rows, depth), lambda i: (i, 0)),
            pl.BlockSpec((rows, columns), lambda i: (i, 0)),
        ],
        out_shape=[
            jax.ShapeDtypeStruct((steps * rows, depth), BF16),
            jax.ShapeDtypeStruct((steps * rows, columns), F32),
        ],
        compiler_params=pltpu.CompilerParams(vmem_limit_bytes=VMEM_LIMIT),
        cost_estimate=pl.CostEstimate(
            flops=2 * steps * rows * depth * columns,
            bytes_accessed=steps * rows * (4 * depth + 4 * columns) + 2 * depth * columns,
            transcendentals=0,
        ),
        name="unpack_and_multiply",
    )(received, weight)


def follow(value, earlier):
    def kernel(value_ref, earlier_ref, out_ref):
        del value_ref, earlier_ref, out_ref

    anywhere = pl.BlockSpec(memory_space=pl.ANY)
    return pl.pallas_call(
        kernel,
        in_specs=[anywhere, anywhere],
        out_specs=anywhere,
        out_shape=jax.ShapeDtypeStruct(value.shape, value.dtype),
        input_output_aliases={0: 0},
        name="follow",
    )(value, earlier)


def contract_rows(left, right):
    return lax.dot_general(left, right, (((0,), (0,)), ((), ())), preferred_element_type=F32)


def per_device(tokens, cotangent, routes, combine_weights, gate_dense, up_dense, down_dense):
    blocks, owners = lax.axis_size("dp"), lax.axis_size(("z", "y"))
    hidden = gate_dense.shape[1] // owners
    everyone = ("dp", "z", "y")
    routes_t, weights_t = routes.T, combine_weights.T

    w_send = pack_weights(gate_dense, up_dense, down_dense, owners)
    w_all = lax.all_to_all(w_send, ("z", "y"), split_axis=0, concat_axis=0, tiled=True)
    w_all = w_all.reshape(-1, w_all.shape[2])
    odd = lax.axis_index(("z", "y")) % 2 == 1
    wide = w_all.shape[1] // 3
    w_gate, w_up, w_down = (
        jnp.where(odd, w_all[:, (n + 1) * wide - hidden : (n + 1) * wide], w_all[:, n * wide : n * wide + hidden])
        for n in range(3)
    )
    w_pair = jnp.concatenate([w_gate, w_up], axis=1)

    def packed(source, scale):
        send = pack_rows(routes_t, weights_t, source, owners, blocks, scale)
        return send.reshape((-1,) + send.shape[2:])

    def exchange(send):
        return lax.all_to_all(send, everyone, split_axis=0, concat_axis=0, tiled=True)

    x_received = exchange(packed(tokens, False))
    x_rows, pair = unpack_and_multiply(x_received, w_pair, owners)
    pair = lax.psum_scatter(pair, "dp", scatter_dimension=0, tiled=True)
    gate_vals, up_vals = pair[:, :hidden], pair[:, hidden:]
    sigma = jax.nn.sigmoid(gate_vals)
    active = gate_vals * sigma
    slope = sigma * (1.0 + gate_vals * (1.0 - sigma))
    hidden_all = lax.all_gather((active * up_vals).astype(BF16), "dp", axis=0, tiled=True)

    dy_rows, back = unpack_and_multiply(
        exchange(follow(packed(cotangent, True), x_received)), w_down, owners
    )
    back = lax.psum_scatter(back, "dp", scatter_dimension=0, tiled=True)
    d_pair = jnp.concatenate(
        [(back * up_vals * slope).astype(BF16), (back * active).astype(BF16)], axis=1
    )
    grad_down = contract_rows(hidden_all, dy_rows).T
    grad_pair = contract_rows(lax.all_gather(d_pair, "dp", axis=0, tiled=True), x_rows)
    return (grad_pair[:hidden].T, grad_pair[hidden:].T, grad_down)


def solution(mesh):
    fine = Mesh(mesh.devices.reshape(mesh.devices.shape[0], -1, 4), ("dp", "z", "y"))
    split = P(("dp", "z", "y"), None)
    return jax.shard_map(
        per_device,
        mesh=fine,
        in_specs=(split,) * 7,
        out_specs=(P("dp", ("z", "y")),) * 3,
        check_vma=False,
    )
```

```python
import jax
import jax.numpy as jnp
from jax import lax
from jax.experimental import pallas as pl
from jax.experimental.pallas import tpu as pltpu
from jax.sharding import PartitionSpec as P

F32 = jnp.float32
BF16 = jnp.bfloat16
VMEM_LIMIT = 48 * 1024 * 1024
ANYWHERE = pl.BlockSpec(memory_space=pl.ANY)


def iota(shape, dim):
    return lax.broadcasted_iota(jnp.int32, shape, dim)


def one_if(mask):
    return jnp.where(mask, 1.0, 0.0).astype(BF16)


def pack_rows(routes_t, weights_t, source, owners, blocks, scale):
    rows, width = source.shape
    part = width // blocks
    tiles = part // 128
    main = owners * 8

    def kernel(routes_ref, weights_ref, source_ref, out_ref, pick_ref, factor_ref):
        @pl.when(pl.program_id(0) == 0)
        def _():
            row = iota((2 * main, rows), 0)
            expert = lax.shift_right_logical(jnp.where(row < main, row, row - main), 3)
            first = routes_ref[0:1, :] == expert
            second = routes_ref[1:2, :] == expert
            named = first | second
            before = one_if(iota((rows, rows), 0) < iota((rows, rows), 1))
            rank = jnp.dot(one_if(named), before, preferred_element_type=F32)
            wanted = jnp.where(row < main, jnp.bitwise_and(row, 7), 8).astype(F32)
            picked = named & (rank == wanted)
            pick_ref[...] = one_if(picked)
            value = jnp.where(first, weights_ref[0:1, :], 0.0) + jnp.where(
                second, weights_ref[1:2, :], 0.0
            )
            factor_ref[...] = jnp.sum(jnp.where(picked, value, 0.0), axis=1, keepdims=True)

        val = jnp.dot(pick_ref[...], source_ref[...], preferred_element_type=F32)
        if scale:
            val = val * factor_ref[...]
        sub = jnp.bitwise_and(iota((main, 128), 0), 7)
        ninth = jnp.zeros((main, 128), F32)
        for j in range(tiles):
            cols = slice(128 * j, 128 * (j + 1))
            out_ref[0, :, 8 * j : 8 * (j + 1), :] = (
                val[:main, cols].reshape(owners, 8, 128).astype(BF16)
            )
            ninth = jnp.where(sub == j, val[main:, cols], ninth)
        out_ref[0, :, 8 * tiles :, :] = ninth.reshape(owners, 8, 128).astype(BF16)

    return pl.pallas_call(
        kernel,
        grid=(blocks,),
        in_specs=[
            pl.BlockSpec((2, rows), lambda i: (0, 0)),
            pl.BlockSpec((2, rows), lambda i: (0, 0)),
            pl.BlockSpec((rows, part), lambda i: (0, i)),
        ],
        out_specs=pl.BlockSpec((1, owners, 9 * tiles, 128), lambda i: (i, 0, 0, 0)),
        out_shape=jax.ShapeDtypeStruct((blocks, owners, 9 * tiles, 128), BF16),
        scratch_shapes=[pltpu.VMEM((2 * main, rows), BF16), pltpu.VMEM((2 * main, 1), F32)],
        compiler_params=pltpu.CompilerParams(vmem_limit_bytes=VMEM_LIMIT),
        cost_estimate=pl.CostEstimate(
            flops=4 * main * rows * width, bytes_accessed=2 * width * (rows + 9 * owners), transcendentals=0
        ),
        name="pack_rows",
    )(routes_t, weights_t, source)


def pack_weights(gate, up, down, owners):
    depth, total = gate.shape
    wide = total // owners
    many = 4
    full = -(-3 * wide // 128) * 128

    def kernel(gate_ref, up_ref, down_ref, out_ref):
        for e in range(many):
            for n, ref in enumerate((gate_ref, up_ref, down_ref)):
                out_ref[e, :, n * wide : (n + 1) * wide] = ref[:, e * wide : (e + 1) * wide]
            out_ref[e, :, 3 * wide :] = jnp.zeros((depth, full - 3 * wide), BF16)

    spec = pl.BlockSpec((depth, many * wide), lambda i: (0, i))
    return pl.pallas_call(
        kernel,
        grid=(owners // many,),
        in_specs=[spec, spec, spec],
        out_specs=pl.BlockSpec((many, depth, full), lambda i: (i, 0, 0)),
        out_shape=jax.ShapeDtypeStruct((owners, depth, full), BF16),
        compiler_params=pltpu.CompilerParams(vmem_limit_bytes=VMEM_LIMIT),
        cost_estimate=pl.CostEstimate(
            flops=0, bytes_accessed=2 * depth * (3 * total + owners * full), transcendentals=0
        ),
        name="pack_weights",
    )(gate, up, down)


def unpack_and_multiply(place, received, weight, chips, first, parts, split):
    senders, height, _ = received.shape
    tiles = height // 9
    depth, columns = weight.shape
    group = senders // (2 * chips)
    main = group * 8
    half = group * 9 // 2

    def kernel(place_ref, received_ref, weight_ref, rows_ref, *refs):
        product_refs, work_ref = refs[:-1], refs[-1]
        core = place_ref[1]
        row, col = iota((main, main), 0), iota((main, main), 1)
        turn = one_if(
            (row % group == lax.shift_right_logical(col, 3)) & (row // group == jnp.bitwise_and(col, 7))
        )
        for j in range(tiles):
            work_ref[:main, 128 * j : 128 * (j + 1)] = (
                received_ref[:, 8 * j : 8 * (j + 1), :].astype(F32).reshape(main, 128).astype(BF16)
            )
        last = received_ref[:, 8 * tiles :, :].astype(F32).reshape(main, 128).astype(BF16)
        ninth = jnp.dot(turn, last, preferred_element_type=F32).astype(BF16)
        for j in range(tiles):
            work_ref[main:, 128 * j : 128 * (j + 1)] = ninth[group * j : group * (j + 1)]
        product = jnp.dot(work_ref[...], weight_ref[...], preferred_element_type=F32)
        low, high = product[:half], product[half:]
        if split:
            product_refs[0][0] = jnp.where(core == 0, low, high)
            product_refs[1][0] = jnp.where(core == 0, high, low)
            rows_ref[0, 0, 0] = work_ref[:half]
            rows_ref[0, 0, 1] = work_ref[half:]
        else:
            product_refs[0][0, 0, 0] = low
            product_refs[0][0, 1, 0] = high
            rows_ref[0, 0, core] = work_ref[:half]
            rows_ref[0, 0, 1 - core] = work_ref[half:]

    def slot(i, place_ref):
        return (place_ref[0] + chips - i % chips) % chips

    if split:
        rows_map = lambda i, s: (i // chips, i % chips, 0, 0, 0)
        product_specs = [pl.BlockSpec((1, half, columns), lambda i, s: (slot(i, s), 0, 0))] * 2
        product_shapes = [jax.ShapeDtypeStruct((chips, half, columns), F32)] * 2
    else:
        rows_map = lambda i, s: (i // chips, slot(i, s), 0, 0, 0)
        product_specs = [
            pl.BlockSpec((1, 2, 1, half, columns), lambda i, s: (i % chips, 0, i // chips, 0, 0))
        ]
        product_shapes = [jax.ShapeDtypeStruct((chips, 2, parts, half, columns), F32)]
    return pl.pallas_call(
        kernel,
        grid_spec=pltpu.PrefetchScalarGridSpec(
            num_scalar_prefetch=1,
            grid=(parts * chips,),
            in_specs=[
                pl.BlockSpec((group, height, 128), lambda i, s: (first * chips + i, 0, 0)),
                pl.BlockSpec((depth, columns), lambda i, s: (0, 0)),
            ],
            out_specs=[pl.BlockSpec((1, 1, 2, half, depth), rows_map)] + product_specs,
            scratch_shapes=[pltpu.VMEM((2 * half, depth), BF16)],
        ),
        out_shape=[jax.ShapeDtypeStruct((parts, chips, 2, half, depth), BF16)] + product_shapes,
        compiler_params=pltpu.CompilerParams(vmem_limit_bytes=VMEM_LIMIT),
        cost_estimate=pl.CostEstimate(
            flops=4 * parts * chips * half * depth * columns,
            bytes_accessed=parts * chips * half * (8 * depth + 8 * columns) + 2 * depth * columns,
            transcendentals=0,
        ),
        name="unpack_and_multiply",
    )(place, received, weight)


def add_steps(one, two, kind):
    steps, rows, columns = one.shape

    def kernel(one_ref, two_ref, *out_refs):
        for n in range(steps):
            out_refs[n][...] = (one_ref[n] + two_ref[n]).astype(out_refs[n].dtype)

    whole = pl.BlockSpec(memory_space=pltpu.VMEM)
    return pl.pallas_call(
        kernel,
        in_specs=[whole] * 2,
        out_specs=[whole] * steps,
        out_shape=[
            jax.ShapeDtypeStruct((rows, columns), kind if n else F32) for n in range(steps)
        ],
        compiler_params=pltpu.CompilerParams(vmem_limit_bytes=VMEM_LIMIT),
        cost_estimate=pl.CostEstimate(
            flops=one.size, bytes_accessed=12 * one.size, transcendentals=0
        ),
        name="add_steps",
    )(one, two)


def follow(values, earlier):
    count = len(values)

    def kernel(*refs):
        del refs

    return pl.pallas_call(
        kernel,
        in_specs=[ANYWHERE] * (count + len(earlier)),
        out_specs=[ANYWHERE] * count,
        out_shape=[jax.ShapeDtypeStruct(v.shape, v.dtype) for v in values],
        input_output_aliases={n: n for n in range(count)},
        name="follow",
    )(*values, *earlier)


def contract_rows(left, right):
    return lax.dot_general(left, right, (((0,), (0,)), ((), ())), preferred_element_type=F32)


def flat(value):
    return value.reshape(-1, value.shape[-1])


def per_device(tokens, cotangent, routes, combine_weights, gate_dense, up_dense, down_dense):
    blocks, owners = lax.axis_size("dp"), lax.axis_size("expert")
    chips = blocks // 2
    hidden = gate_dense.shape[1] // owners
    routes_t, weights_t = routes.T, combine_weights.T
    dp = lax.axis_index("dp")
    place = jnp.stack([dp // 2, dp % 2]).astype(jnp.int32)

    def along_x(step, value):
        if step % chips == 0:
            return value
        pairs = [(2 * i + c, 2 * ((i + step) % chips) + c) for i in range(chips) for c in range(2)]
        return lax.ppermute(value, "dp", pairs)

    def other_core(value):
        return lax.ppermute(value, "dp", [(i, i ^ 1) for i in range(blocks)])

    def packed(source, scale):
        return pack_rows(routes_t, weights_t, source, owners, blocks, scale)

    def exchange(send):
        send = send.reshape((-1,) + send.shape[-2:])
        return lax.all_to_all(send, ("dp", "expert"), split_axis=0, concat_axis=0, tiled=True)

    def reduce_rows(keep, send):
        sums = add_steps(keep, other_core(send), BF16)
        total = sums[0]
        for step in range(1, chips):
            total = total + along_x(-step, sums[step]).astype(F32)
        return total

    def gather_rows(value):
        pieces = []
        for step in range(chips):
            piece = along_x(step, value)
            pieces += [piece, other_core(piece)]
        return jnp.concatenate(pieces, axis=0)

    w_send = pack_weights(gate_dense, up_dense, down_dense, owners)
    w_all = flat(lax.all_to_all(w_send, "expert", split_axis=0, concat_axis=0, tiled=True))
    w_pair, w_down = w_all[:, : 2 * hidden], w_all[:, 2 * hidden : 3 * hidden]

    dy_send = packed(cotangent, True)
    (x_send,) = follow([packed(tokens, False)], [dy_send])
    x_received = exchange(x_send)
    dy_received = exchange(dy_send)

    x_rows, pair = unpack_and_multiply(place, x_received, w_pair, chips, 0, 2, False)
    pair = lax.psum_scatter(flat(pair), "dp", scatter_dimension=0, tiled=True)
    gate_vals, up_vals = pair[:, :hidden], pair[:, hidden:]
    sigma = jax.nn.sigmoid(gate_vals)
    active = gate_vals * sigma
    slope = up_vals * (sigma * (1.0 + gate_vals * (1.0 - sigma)))
    hidden_mine = (active * up_vals).astype(BF16)
    hidden_all = lax.all_gather(hidden_mine, "dp", axis=0, tiled=True)
    hidden_all = hidden_all.reshape(blocks, 2, -1, hidden)

    half = pair.shape[0] // 2
    grads = None
    for n in range(2):
        if n == 1:
            (dy_received,) = follow([dy_received], [hidden_mine])
        dy_rows, keep, send = unpack_and_multiply(place, dy_received, w_down, chips, n, 1, True)
        back = reduce_rows(keep, send)
        mine = slice(n * half, (n + 1) * half)
        d_pair = jnp.concatenate(
            [(back * slope[mine]).astype(BF16), (back * active[mine]).astype(BF16)], axis=1
        )
        grad_down = contract_rows(flat(hidden_all[:, n]), flat(dy_rows))
        grad_pair = contract_rows(gather_rows(d_pair), flat(x_rows[n]))
        grads = (grad_pair, grad_down) if grads is None else (grads[0] + grad_pair, grads[1] + grad_down)
    return (grads[0][:hidden].T, grads[0][hidden:].T, grads[1].T)


def solution(mesh):
    split = P(("dp", "expert"), None)
    return jax.shard_map(
        per_device,
        mesh=mesh,
        in_specs=(split,) * 7,
        out_specs=(P("dp", "expert"),) * 3,
        check_vma=False,
    )
```

```python
import jax
import jax.numpy as jnp
from jax import lax
from jax.experimental import pallas as pl
from jax.experimental.pallas import tpu as pltpu
from jax.sharding import PartitionSpec as P

F32 = jnp.float32
BF16 = jnp.bfloat16
VMEM_LIMIT = 20 * 1024 * 1024
ANYWHERE = pl.BlockSpec(memory_space=pl.ANY)


def iota(shape, dim):
    return lax.broadcasted_iota(jnp.int32, shape, dim)


def one_if(mask):
    return jnp.where(mask, 1.0, 0.0).astype(BF16)


def pack_rows(routes_t, weights_t, source, owners, blocks, scale):
    rows, width = source.shape
    part = width // blocks
    tiles = part // 128
    main = owners * 8

    def kernel(routes_ref, weights_ref, source_ref, out_ref, pick_ref, factor_ref):
        @pl.when(pl.program_id(0) == 0)
        def _():
            row = iota((2 * main, rows), 0)
            expert = lax.shift_right_logical(jnp.where(row < main, row, row - main), 3)
            first = routes_ref[0:1, :] == expert
            second = routes_ref[1:2, :] == expert
            named = first | second
            before = one_if(iota((rows, rows), 0) < iota((rows, rows), 1))
            rank = jnp.dot(one_if(named), before, preferred_element_type=F32)
            wanted = jnp.where(row < main, jnp.bitwise_and(row, 7), 8).astype(F32)
            picked = named & (rank == wanted)
            pick_ref[...] = one_if(picked)
            value = jnp.where(first, weights_ref[0:1, :], 0.0) + jnp.where(
                second, weights_ref[1:2, :], 0.0
            )
            factor_ref[...] = jnp.sum(jnp.where(picked, value, 0.0), axis=1, keepdims=True)

        val = jnp.dot(pick_ref[...], source_ref[...], preferred_element_type=F32)
        if scale:
            val = val * factor_ref[...]
        sub = jnp.bitwise_and(iota((main, 128), 0), 7)
        ninth = jnp.zeros((main, 128), F32)
        for j in range(tiles):
            cols = slice(128 * j, 128 * (j + 1))
            out_ref[0, :, 8 * j : 8 * (j + 1), :] = (
                val[:main, cols].reshape(owners, 8, 128).astype(BF16)
            )
            ninth = jnp.where(sub == j, val[main:, cols], ninth)
        out_ref[0, :, 8 * tiles :, :] = ninth.reshape(owners, 8, 128).astype(BF16)

    return pl.pallas_call(
        kernel,
        grid=(blocks,),
        in_specs=[
            pl.BlockSpec((2, rows), lambda i: (0, 0)),
            pl.BlockSpec((2, rows), lambda i: (0, 0)),
            pl.BlockSpec((rows, part), lambda i: (0, i)),
        ],
        out_specs=pl.BlockSpec((1, owners, 9 * tiles, 128), lambda i: (i, 0, 0, 0)),
        out_shape=jax.ShapeDtypeStruct((blocks, owners, 9 * tiles, 128), BF16),
        scratch_shapes=[pltpu.VMEM((2 * main, rows), BF16), pltpu.VMEM((2 * main, 1), F32)],
        compiler_params=pltpu.CompilerParams(vmem_limit_bytes=3 * VMEM_LIMIT),
        cost_estimate=pl.CostEstimate(
            flops=4 * main * rows * width, bytes_accessed=2 * width * (rows + 9 * owners), transcendentals=0
        ),
        name="pack_rows",
    )(routes_t, weights_t, source)


def pack_weights(gate, up, down, owners):
    depth, total = gate.shape
    wide = total // owners
    many = 4
    full = -(-3 * wide // 128) * 128

    def kernel(gate_ref, up_ref, down_ref, out_ref):
        for e in range(many):
            for n, ref in enumerate((gate_ref, up_ref, down_ref)):
                out_ref[e, :, n * wide : (n + 1) * wide] = ref[:, e * wide : (e + 1) * wide]
            out_ref[e, :, 3 * wide :] = jnp.zeros((depth, full - 3 * wide), BF16)

    spec = pl.BlockSpec((depth, many * wide), lambda i: (0, i))
    return pl.pallas_call(
        kernel,
        grid=(owners // many,),
        in_specs=[spec, spec, spec],
        out_specs=pl.BlockSpec((many, depth, full), lambda i: (i, 0, 0)),
        out_shape=jax.ShapeDtypeStruct((owners, depth, full), BF16),
        compiler_params=pltpu.CompilerParams(vmem_limit_bytes=3 * VMEM_LIMIT),
        cost_estimate=pl.CostEstimate(
            flops=0, bytes_accessed=2 * depth * (3 * total + owners * full), transcendentals=0
        ),
        name="pack_weights",
    )(gate, up, down)


def unpack_and_multiply(place, received, weight, chips, first, parts):
    senders, height, _ = received.shape
    tiles = height // 9
    depth, columns = weight.shape
    group = senders // (2 * chips)
    main = group * 8
    half = group * 9 // 2

    def kernel(place_ref, received_ref, weight_ref, rows_ref, keep_ref, send_ref, work_ref):
        core = place_ref[1]
        row, col = iota((main, main), 0), iota((main, main), 1)
        turn = one_if(
            (row % group == lax.shift_right_logical(col, 3)) & (row // group == jnp.bitwise_and(col, 7))
        )
        for j in range(tiles):
            work_ref[:main, 128 * j : 128 * (j + 1)] = (
                received_ref[:, 8 * j : 8 * (j + 1), :].astype(F32).reshape(main, 128).astype(BF16)
            )
        last = received_ref[:, 8 * tiles :, :].astype(F32).reshape(main, 128).astype(BF16)
        ninth = jnp.dot(turn, last, preferred_element_type=F32).astype(BF16)
        for j in range(tiles):
            work_ref[main:, 128 * j : 128 * (j + 1)] = ninth[group * j : group * (j + 1)]
        product = jnp.dot(work_ref[...], weight_ref[...], preferred_element_type=F32)
        low, high = product[:half], product[half:]
        keep_ref[0, 0] = jnp.where(core == 0, low, high)
        send_ref[0, 0] = jnp.where(core == 0, high, low)
        rows_ref[0, 0, core] = work_ref[:half]
        rows_ref[0, 0, 1 - core] = work_ref[half:]

    def slot(i, place_ref):
        return (place_ref[0] + chips - i % chips) % chips

    product_spec = pl.BlockSpec((1, 1, half, columns), lambda i, s: (slot(i, s), i // chips, 0, 0))
    product_shape = jax.ShapeDtypeStruct((chips, parts, half, columns), F32)
    return pl.pallas_call(
        kernel,
        grid_spec=pltpu.PrefetchScalarGridSpec(
            num_scalar_prefetch=1,
            grid=(parts * chips,),
            in_specs=[
                pl.BlockSpec((group, height, 128), lambda i, s: (first * chips + i, 0, 0)),
                pl.BlockSpec((depth, columns), lambda i, s: (0, 0)),
            ],
            out_specs=[
                pl.BlockSpec((1, 1, 2, half, depth), lambda i, s: (i // chips, slot(i, s), 0, 0, 0)),
                product_spec,
                product_spec,
            ],
            scratch_shapes=[pltpu.VMEM((2 * half, depth), BF16)],
        ),
        out_shape=[
            jax.ShapeDtypeStruct((parts, chips, 2, half, depth), BF16),
            product_shape,
            product_shape,
        ],
        compiler_params=pltpu.CompilerParams(vmem_limit_bytes=VMEM_LIMIT),
        cost_estimate=pl.CostEstimate(
            flops=4 * parts * chips * half * depth * columns,
            bytes_accessed=parts * chips * half * (8 * depth + 8 * columns) + 2 * depth * columns,
            transcendentals=0,
        ),
        name="unpack_and_multiply",
    )(place, received, weight)


def add_steps(one, two, kind):
    steps, rows, columns = one.shape

    def kernel(one_ref, two_ref, *out_refs):
        for n in range(steps):
            out_refs[n][...] = (one_ref[n] + two_ref[n]).astype(out_refs[n].dtype)

    whole = pl.BlockSpec(memory_space=pltpu.VMEM)
    return pl.pallas_call(
        kernel,
        in_specs=[whole] * 2,
        out_specs=[whole] * steps,
        out_shape=[
            jax.ShapeDtypeStruct((rows, columns), kind if n else F32) for n in range(steps)
        ],
        compiler_params=pltpu.CompilerParams(vmem_limit_bytes=VMEM_LIMIT),
        cost_estimate=pl.CostEstimate(
            flops=one.size, bytes_accessed=12 * one.size, transcendentals=0
        ),
        name="add_steps",
    )(one, two)


def slopes(total, active, slope, part):
    own, others = total[0], total[1:]
    rows, columns = own.shape

    def kernel(own_ref, *refs):
        active_ref, slope_ref, out_ref = refs[len(others) :]
        back = own_ref[...]
        for ref in refs[: len(others)]:
            back = back + ref[...].astype(F32)
        out_ref[:, :columns] = (back * slope_ref[...]).astype(BF16)
        out_ref[:, columns:] = (back * active_ref[...]).astype(BF16)

    whole = pl.BlockSpec((rows, columns), lambda i: (0, 0))
    mine = pl.BlockSpec((rows, columns), lambda i: (part, 0))
    return pl.pallas_call(
        kernel,
        grid=(1,),
        in_specs=[whole] * len(total) + [mine] * 2,
        out_specs=pl.BlockSpec((rows, 2 * columns), lambda i: (0, 0)),
        out_shape=jax.ShapeDtypeStruct((rows, 2 * columns), BF16),
        compiler_params=pltpu.CompilerParams(vmem_limit_bytes=VMEM_LIMIT),
        cost_estimate=pl.CostEstimate(
            flops=6 * own.size, bytes_accessed=24 * own.size, transcendentals=0
        ),
        name="slopes",
    )(own, *others, active, slope)


def follow(values, earlier):
    count = len(values)

    def kernel(*refs):
        del refs

    return pl.pallas_call(
        kernel,
        in_specs=[ANYWHERE] * (count + len(earlier)),
        out_specs=[ANYWHERE] * count,
        out_shape=[jax.ShapeDtypeStruct(v.shape, v.dtype) for v in values],
        input_output_aliases={n: n for n in range(count)},
        name="follow",
    )(*values, *earlier)


def contract_rows(pieces, rows):
    parts, chips, cores, half, depth = rows.shape
    columns = pieces[0].shape[1]
    outs = 1 + columns // 896
    hidden = columns // outs
    count = len(pieces)
    height = parts * count * half
    wide = 256

    def kernel(*refs):
        piece_refs, rows_ref = refs[:count], refs[count]
        out_refs, done_ref = refs[count + 1 : -3], refs[-3]
        left_ref, turned_ref = refs[-2:]
        done_ref[...] = jnp.zeros_like(done_ref)

        @pl.when(pl.program_id(0) == 0)
        def _():
            for p in range(parts):
                for n in range(count):
                    to = (p * count + n) * half
                    left_ref[to : to + half] = piece_refs[n][p * half : (p + 1) * half]
            turned_ref[...] = left_ref[...].T

        right = rows_ref[...].reshape(height, wide)
        product = jnp.dot(turned_ref[...], right, preferred_element_type=F32)
        for n in range(outs):
            out_refs[n][...] = product[n * hidden : (n + 1) * hidden]

    return pl.pallas_call(
        kernel,
        grid=(depth // wide,),
        in_specs=[pl.BlockSpec(piece.shape, lambda i: (0, 0)) for piece in pieces]
        + [pl.BlockSpec(rows.shape[:4] + (wide,), lambda i: (0, 0, 0, 0, i))],
        out_specs=[pl.BlockSpec((hidden, wide), lambda i: (0, i))] * outs
        + [pl.BlockSpec((8, 128), lambda i: (0, 0))],
        out_shape=[jax.ShapeDtypeStruct((hidden, depth), F32)] * outs
        + [jax.ShapeDtypeStruct((8, 128), F32)],
        scratch_shapes=[pltpu.VMEM((height, columns), BF16), pltpu.VMEM((columns, height), BF16)],
        compiler_params=pltpu.CompilerParams(vmem_limit_bytes=3 * VMEM_LIMIT),
        cost_estimate=pl.CostEstimate(
            flops=2 * height * depth * columns,
            bytes_accessed=2 * height * (depth + columns) + 4 * columns * depth,
            transcendentals=0,
        ),
        name="contract_rows",
    )(*pieces, rows)


def flat(value):
    return value.reshape(-1, value.shape[-1])


def per_device(tokens, cotangent, routes, combine_weights, gate_dense, up_dense, down_dense):
    blocks, owners = lax.axis_size("dp"), lax.axis_size("expert")
    chips = blocks // 2
    hidden = gate_dense.shape[1] // owners
    routes_t, weights_t = routes.T, combine_weights.T
    dp = lax.axis_index("dp")
    place = jnp.stack([dp // 2, dp % 2]).astype(jnp.int32)

    def along_x(step, value):
        if step % chips == 0:
            return value
        pairs = [(2 * i + c, 2 * ((i + step) % chips) + c) for i in range(chips) for c in range(2)]
        return lax.ppermute(value, "dp", pairs)

    def other_core(value):
        return lax.ppermute(value, "dp", [(i, i ^ 1) for i in range(blocks)])

    def packed(source, scale):
        return pack_rows(routes_t, weights_t, source, owners, blocks, scale)

    def exchange(send):
        send = send.reshape((-1,) + send.shape[-2:])
        return lax.all_to_all(send, ("dp", "expert"), split_axis=0, concat_axis=0, tiled=True)

    def reduce_rows(keep, send):
        keep, send = (value.reshape(chips, -1, value.shape[-1]) for value in (keep, send))
        sums = add_steps(keep, other_core(send), BF16)
        return [sums[0]] + [along_x(-step, sums[step]) for step in range(1, chips)]

    def gather_rows(value, after=()):
        pieces = []
        for step in range(chips):
            piece = along_x(step, value)
            if after and step == chips - 1:
                (piece,) = follow([piece], after)
            pieces += [piece, other_core(piece)]
        return pieces

    w_send = pack_weights(gate_dense, up_dense, down_dense, owners)
    w_all = flat(lax.all_to_all(w_send, "expert", split_axis=0, concat_axis=0, tiled=True))
    w_pair, w_down = w_all[:, : 2 * hidden], w_all[:, 2 * hidden : 3 * hidden]

    dy_send = packed(cotangent, True)
    (x_send,) = follow([packed(tokens, False)], [dy_send])
    x_received = exchange(x_send)
    dy_received = exchange(dy_send)

    x_rows, keep, send = unpack_and_multiply(place, x_received, w_pair, chips, 0, 2)
    pair = sum(total.astype(F32) for total in reduce_rows(keep, send))
    gate_vals, up_vals = pair[:, :hidden], pair[:, hidden:]
    sigma = jax.nn.sigmoid(gate_vals)
    active = gate_vals * sigma
    slope = up_vals * (sigma * (1.0 + gate_vals * (1.0 - sigma)))
    hidden_all = gather_rows((active * up_vals).astype(BF16))
    (dy_received,) = follow([dy_received], hidden_all)

    dy_rows, keep, send = unpack_and_multiply(place, dy_received, w_down, chips, 0, 2)
    d_pair = slopes(reduce_rows(keep, send), active, slope, 0)
    grad_down, down_done = contract_rows(hidden_all, dy_rows)
    grad_gate, grad_up, _ = contract_rows(gather_rows(d_pair, [down_done]), x_rows)
    return (grad_gate.T, grad_up.T, grad_down.T)


def solution(mesh):
    split = P(("dp", "expert"), None)
    return jax.shard_map(
        per_device,
        mesh=mesh,
        in_specs=(split,) * 7,
        out_specs=(P("dp", "expert"),) * 3,
        check_vma=False,
    )
```

```python
import jax
import jax.numpy as jnp
from jax import lax
from jax.experimental import pallas as pl
from jax.experimental.pallas import tpu as pltpu
from jax.sharding import PartitionSpec as P

F32 = jnp.float32
BF16 = jnp.bfloat16
VMEM_LIMIT = 20 * 1024 * 1024
ANYWHERE = pl.BlockSpec(memory_space=pl.ANY)


def iota(shape, dim):
    return lax.broadcasted_iota(jnp.int32, shape, dim)


def one_if(mask):
    return jnp.where(mask, 1.0, 0.0).astype(BF16)


def pack_rows(routes_t, weights_t, source, owners, blocks, scale):
    rows, width = source.shape
    part = width // blocks
    tiles = part // 128
    main = owners * 8

    def kernel(routes_ref, weights_ref, source_ref, out_ref, pick_ref, factor_ref):
        @pl.when(pl.program_id(0) == 0)
        def _():
            row = iota((2 * main, rows), 0)
            expert = lax.shift_right_logical(jnp.where(row < main, row, row - main), 3)
            first = routes_ref[0:1, :] == expert
            second = routes_ref[1:2, :] == expert
            named = first | second
            before = one_if(iota((rows, rows), 0) < iota((rows, rows), 1))
            rank = jnp.dot(one_if(named), before, preferred_element_type=F32)
            wanted = jnp.where(row < main, jnp.bitwise_and(row, 7), 8).astype(F32)
            picked = named & (rank == wanted)
            pick_ref[...] = one_if(picked)
            value = jnp.where(first, weights_ref[0:1, :], 0.0) + jnp.where(
                second, weights_ref[1:2, :], 0.0
            )
            factor_ref[...] = jnp.sum(jnp.where(picked, value, 0.0), axis=1, keepdims=True)

        val = jnp.dot(pick_ref[...], source_ref[...], preferred_element_type=F32)
        if scale:
            val = val * factor_ref[...]
        sub = jnp.bitwise_and(iota((main, 128), 0), 7)
        ninth = jnp.zeros((main, 128), F32)
        for j in range(tiles):
            cols = slice(128 * j, 128 * (j + 1))
            out_ref[0, :, 8 * j : 8 * (j + 1), :] = (
                val[:main, cols].reshape(owners, 8, 128).astype(BF16)
            )
            ninth = jnp.where(sub == j, val[main:, cols], ninth)
        out_ref[0, :, 8 * tiles :, :] = ninth.reshape(owners, 8, 128).astype(BF16)

    return pl.pallas_call(
        kernel,
        grid=(blocks,),
        in_specs=[
            pl.BlockSpec((2, rows), lambda i: (0, 0)),
            pl.BlockSpec((2, rows), lambda i: (0, 0)),
            pl.BlockSpec((rows, part), lambda i: (0, i)),
        ],
        out_specs=pl.BlockSpec((1, owners, 9 * tiles, 128), lambda i: (i, 0, 0, 0)),
        out_shape=jax.ShapeDtypeStruct((blocks, owners, 9 * tiles, 128), BF16),
        scratch_shapes=[pltpu.VMEM((2 * main, rows), BF16), pltpu.VMEM((2 * main, 1), F32)],
        compiler_params=pltpu.CompilerParams(vmem_limit_bytes=3 * VMEM_LIMIT),
        cost_estimate=pl.CostEstimate(
            flops=4 * main * rows * width, bytes_accessed=2 * width * (rows + 9 * owners), transcendentals=0
        ),
        name="pack_rows",
    )(routes_t, weights_t, source)


def pack_weights(gate, up, down, owners):
    depth, total = gate.shape
    wide = total // owners
    many = 4
    full = -(-3 * wide // 128) * 128

    def kernel(gate_ref, up_ref, down_ref, out_ref):
        for e in range(many):
            for n, ref in enumerate((gate_ref, up_ref, down_ref)):
                out_ref[e, :, n * wide : (n + 1) * wide] = ref[:, e * wide : (e + 1) * wide]
            out_ref[e, :, 3 * wide :] = jnp.zeros((depth, full - 3 * wide), BF16)

    spec = pl.BlockSpec((depth, many * wide), lambda i: (0, i))
    return pl.pallas_call(
        kernel,
        grid=(owners // many,),
        in_specs=[spec, spec, spec],
        out_specs=pl.BlockSpec((many, depth, full), lambda i: (i, 0, 0)),
        out_shape=jax.ShapeDtypeStruct((owners, depth, full), BF16),
        compiler_params=pltpu.CompilerParams(vmem_limit_bytes=3 * VMEM_LIMIT),
        cost_estimate=pl.CostEstimate(
            flops=0, bytes_accessed=2 * depth * (3 * total + owners * full), transcendentals=0
        ),
        name="pack_weights",
    )(gate, up, down)


def unpack_and_multiply(place, received, weight, chips, first, parts):
    senders, height, _ = received.shape
    tiles = height // 9
    depth, columns = weight.shape
    group = senders // (2 * chips)
    main = group * 8
    half = group * 9 // 2

    def kernel(place_ref, received_ref, weight_ref, rows_ref, keep_ref, send_ref, work_ref):
        core = place_ref[1]
        row, col = iota((main, main), 0), iota((main, main), 1)
        turn = one_if(
            (row % group == lax.shift_right_logical(col, 3)) & (row // group == jnp.bitwise_and(col, 7))
        )
        for j in range(tiles):
            work_ref[:main, 128 * j : 128 * (j + 1)] = (
                received_ref[:, 8 * j : 8 * (j + 1), :].astype(F32).reshape(main, 128).astype(BF16)
            )
        last = received_ref[:, 8 * tiles :, :].astype(F32).reshape(main, 128).astype(BF16)
        ninth = jnp.dot(turn, last, preferred_element_type=F32).astype(BF16)
        for j in range(tiles):
            work_ref[main:, 128 * j : 128 * (j + 1)] = ninth[group * j : group * (j + 1)]
        product = jnp.dot(work_ref[...], weight_ref[...], preferred_element_type=F32)
        low, high = product[:half], product[half:]
        keep_ref[0, 0] = jnp.where(core == 0, low, high)
        send_ref[0, 0] = jnp.where(core == 0, high, low)
        rows_ref[0, 0, core] = work_ref[:half]
        rows_ref[0, 0, 1 - core] = work_ref[half:]

    def slot(i, place_ref):
        return (place_ref[0] + chips - i % chips) % chips

    product_spec = pl.BlockSpec((1, 1, half, columns), lambda i, s: (slot(i, s), i // chips, 0, 0))
    product_shape = jax.ShapeDtypeStruct((chips, parts, half, columns), F32)
    return pl.pallas_call(
        kernel,
        grid_spec=pltpu.PrefetchScalarGridSpec(
            num_scalar_prefetch=1,
            grid=(parts * chips,),
            in_specs=[
                pl.BlockSpec((group, height, 128), lambda i, s: (first * chips + i, 0, 0)),
                pl.BlockSpec((depth, columns), lambda i, s: (0, 0)),
            ],
            out_specs=[
                pl.BlockSpec((1, 1, 2, half, depth), lambda i, s: (i // chips, slot(i, s), 0, 0, 0)),
                product_spec,
                product_spec,
            ],
            scratch_shapes=[pltpu.VMEM((2 * half, depth), BF16)],
        ),
        out_shape=[
            jax.ShapeDtypeStruct((parts, chips, 2, half, depth), BF16),
            product_shape,
            product_shape,
        ],
        compiler_params=pltpu.CompilerParams(vmem_limit_bytes=VMEM_LIMIT),
        cost_estimate=pl.CostEstimate(
            flops=4 * parts * chips * half * depth * columns,
            bytes_accessed=parts * chips * half * (8 * depth + 8 * columns) + 2 * depth * columns,
            transcendentals=0,
        ),
        name="unpack_and_multiply",
    )(place, received, weight)


def add_steps(one, two, kind):
    steps, rows, columns = one.shape

    def kernel(one_ref, two_ref, *out_refs):
        for n in range(steps):
            out_refs[n][...] = (one_ref[n] + two_ref[n]).astype(out_refs[n].dtype)

    whole = pl.BlockSpec(memory_space=pltpu.VMEM)
    return pl.pallas_call(
        kernel,
        in_specs=[whole] * 2,
        out_specs=[whole] * steps,
        out_shape=[
            jax.ShapeDtypeStruct((rows, columns), kind if n else F32) for n in range(steps)
        ],
        compiler_params=pltpu.CompilerParams(vmem_limit_bytes=VMEM_LIMIT),
        cost_estimate=pl.CostEstimate(
            flops=one.size, bytes_accessed=12 * one.size, transcendentals=0
        ),
        name="add_steps",
    )(one, two)


def slopes(total, active, slope, part):
    own, others = total[0], total[1:]
    rows, columns = own.shape

    def kernel(own_ref, *refs):
        active_ref, slope_ref, out_ref = refs[len(others) :]
        back = own_ref[...]
        for ref in refs[: len(others)]:
            back = back + ref[...].astype(F32)
        out_ref[:, :columns] = (back * slope_ref[...]).astype(BF16)
        out_ref[:, columns:] = (back * active_ref[...]).astype(BF16)

    whole = pl.BlockSpec((rows, columns), lambda i: (0, 0))
    mine = pl.BlockSpec((rows, columns), lambda i: (part, 0))
    return pl.pallas_call(
        kernel,
        grid=(1,),
        in_specs=[whole] * len(total) + [mine] * 2,
        out_specs=pl.BlockSpec((rows, 2 * columns), lambda i: (0, 0)),
        out_shape=jax.ShapeDtypeStruct((rows, 2 * columns), BF16),
        compiler_params=pltpu.CompilerParams(vmem_limit_bytes=VMEM_LIMIT),
        cost_estimate=pl.CostEstimate(
            flops=6 * own.size, bytes_accessed=24 * own.size, transcendentals=0
        ),
        name="slopes",
    )(own, *others, active, slope)


def follow(values, earlier):
    count = len(values)

    def kernel(*refs):
        del refs

    return pl.pallas_call(
        kernel,
        in_specs=[ANYWHERE] * (count + len(earlier)),
        out_specs=[ANYWHERE] * count,
        out_shape=[jax.ShapeDtypeStruct(v.shape, v.dtype) for v in values],
        input_output_aliases={n: n for n in range(count)},
        name="follow",
    )(*values, *earlier)


def contract_rows(pieces, plan, rows, slots, sums=()):
    parts, _, cores, half, depth = rows.shape
    columns = pieces[0].shape[1]
    outs = 1 + columns // 896
    hidden = columns // outs
    count, many = len(pieces), len(slots)
    height = len(plan) * half
    wide = 256

    def kernel(*refs):
        piece_refs, rows_refs = refs[:count], refs[count : count + many]
        sum_refs, out_refs = refs[count + many : -3 - outs], refs[-3 - outs : -3]
        done_ref, left_ref, turned_ref = refs[-3:]
        done_ref[...] = jnp.zeros_like(done_ref)

        @pl.when(pl.program_id(0) == 0)
        def _():
            for n, (piece, first) in enumerate(plan):
                left_ref[n * half : (n + 1) * half] = piece_refs[piece][first : first + half]
            turned_ref[...] = left_ref[...].T

        right = jnp.concatenate([ref[...].reshape(height // many, wide) for ref in rows_refs], axis=0)
        product = jnp.dot(turned_ref[...], right, preferred_element_type=F32)
        for n in range(outs):
            share = product[n * hidden : (n + 1) * hidden]
            out_refs[n][...] = share + sum_refs[n][...] if sums else share

    def rows_spec(slot):
        return pl.BlockSpec((parts, 1, cores, half, wide), lambda i: (0, slot, 0, 0, i))

    tile = pl.BlockSpec((hidden, wide), lambda i: (0, i))
    return pl.pallas_call(
        kernel,
        grid=(depth // wide,),
        in_specs=[pl.BlockSpec(piece.shape, lambda i: (0, 0)) for piece in pieces]
        + [rows_spec(slot) for slot in slots]
        + [tile] * len(sums),
        out_specs=[tile] * outs + [pl.BlockSpec((8, 128), lambda i: (0, 0))],
        out_shape=[jax.ShapeDtypeStruct((hidden, depth), F32)] * outs
        + [jax.ShapeDtypeStruct((8, 128), F32)],
        scratch_shapes=[pltpu.VMEM((height, columns), BF16), pltpu.VMEM((columns, height), BF16)],
        compiler_params=pltpu.CompilerParams(vmem_limit_bytes=3 * VMEM_LIMIT),
        cost_estimate=pl.CostEstimate(
            flops=2 * height * depth * columns,
            bytes_accessed=2 * height * (depth + columns) + 4 * columns * depth,
            transcendentals=0,
        ),
        name="contract_rows",
    )(*pieces, *[rows] * many, *sums)


def flat(value):
    return value.reshape(-1, value.shape[-1])


def per_device(tokens, cotangent, routes, combine_weights, gate_dense, up_dense, down_dense):
    blocks, owners = lax.axis_size("dp"), lax.axis_size("expert")
    chips = blocks // 2
    hidden = gate_dense.shape[1] // owners
    routes_t, weights_t = routes.T, combine_weights.T
    dp = lax.axis_index("dp")
    place = jnp.stack([dp // 2, dp % 2]).astype(jnp.int32)

    def along_x(step, value):
        if step % chips == 0:
            return value
        pairs = [(2 * i + c, 2 * ((i + step) % chips) + c) for i in range(chips) for c in range(2)]
        return lax.ppermute(value, "dp", pairs)

    def other_core(value):
        return lax.ppermute(value, "dp", [(i, i ^ 1) for i in range(blocks)])

    def packed(source, scale):
        return pack_rows(routes_t, weights_t, source, owners, blocks, scale)

    def exchange(send):
        send = send.reshape((-1,) + send.shape[-2:])
        return lax.all_to_all(send, ("dp", "expert"), split_axis=0, concat_axis=0, tiled=True)

    def reduce_rows(keep, send):
        keep, send = (value.reshape(chips, -1, value.shape[-1]) for value in (keep, send))
        sums = add_steps(keep, other_core(send), BF16)
        return [sums[0]] + [along_x(-step, sums[step]) for step in range(1, chips)]

    def gather_rows(value):
        pieces = []
        for step in range(chips):
            piece = along_x(step, value)
            pieces += [piece, other_core(piece)]
        return pieces

    def blocks_of(count):
        return [(2 * n + q, p * half) for n in range(count) for p in range(2) for q in range(2)]

    w_send = pack_weights(gate_dense, up_dense, down_dense, owners)
    w_all = flat(lax.all_to_all(w_send, "expert", split_axis=0, concat_axis=0, tiled=True))
    w_pair, w_down = w_all[:, : 2 * hidden], w_all[:, 2 * hidden : 3 * hidden]

    dy_send = packed(cotangent, True)
    (x_send,) = follow([packed(tokens, False)], [dy_send])
    x_received = exchange(x_send)
    dy_received = exchange(dy_send)

    x_rows, keep, send = unpack_and_multiply(place, x_received, w_pair, chips, 0, 2)
    pair = sum(total.astype(F32) for total in reduce_rows(keep, send))
    gate_vals, up_vals = pair[:, :hidden], pair[:, hidden:]
    sigma = jax.nn.sigmoid(gate_vals)
    active = gate_vals * sigma
    slope = up_vals * (sigma * (1.0 + gate_vals * (1.0 - sigma)))
    hidden_all = gather_rows((active * up_vals).astype(BF16))
    (dy_received,) = follow([dy_received], hidden_all)

    dy_rows, keep, send = unpack_and_multiply(place, dy_received, w_down, chips, 0, 2)
    d_pair = slopes(reduce_rows(keep, send), active, slope, 0)
    half = x_rows.shape[3]
    left, right = along_x(1, d_pair), along_x(-1, d_pair)
    grad_down, down_done = contract_rows(hidden_all, blocks_of(chips), dy_rows, range(chips))
    left, right = follow([left, right], [down_done])
    far = [along_x(1, left[:half]), along_x(-1, right[half:])]
    near = []
    for piece in (d_pair, left, right):
        near += [piece, other_core(piece)]
    *grad_pair, near_done = contract_rows(near, blocks_of(3), x_rows, (0, 1, 3))
    far_left, far_right = follow(far, [near_done])
    far = [far_left, other_core(far_left), far_right, other_core(far_right)]
    grad_gate, grad_up, _ = contract_rows(far, [(n, 0) for n in range(4)], x_rows, (2,), grad_pair)
    return (grad_gate.T, grad_up.T, grad_down.T)


def solution(mesh):
    split = P(("dp", "expert"), None)
    return jax.shard_map(
        per_device,
        mesh=mesh,
        in_specs=(split,) * 7,
        out_specs=(P("dp", "expert"),) * 3,
        check_vma=False,
    )
```

```python
import jax
import jax.numpy as jnp
from jax import lax
from jax.experimental import pallas as pl
from jax.experimental.pallas import tpu as pltpu
from jax.sharding import PartitionSpec as P

F32 = jnp.float32
BF16 = jnp.bfloat16
VMEM_LIMIT = 20 * 1024 * 1024
ANYWHERE = pl.BlockSpec(memory_space=pl.ANY)


def iota(shape, dim):
    return lax.broadcasted_iota(jnp.int32, shape, dim)


def one_if(mask):
    return jnp.where(mask, 1.0, 0.0).astype(BF16)


def pack_rows(routes_t, weights_t, source, owners, blocks, scale):
    rows, width = source.shape
    part = width // blocks
    tiles = part // 128
    main = owners * 8

    def kernel(routes_ref, weights_ref, source_ref, out_ref, pick_ref, factor_ref):
        @pl.when(pl.program_id(0) == 0)
        def _():
            row = iota((2 * main, rows), 0)
            expert = lax.shift_right_logical(jnp.where(row < main, row, row - main), 3)
            first = routes_ref[0:1, :] == expert
            second = routes_ref[1:2, :] == expert
            named = first | second
            before = one_if(iota((rows, rows), 0) < iota((rows, rows), 1))
            rank = jnp.dot(one_if(named), before, preferred_element_type=F32)
            wanted = jnp.where(row < main, jnp.bitwise_and(row, 7), 8).astype(F32)
            picked = named & (rank == wanted)
            pick_ref[...] = one_if(picked)
            value = jnp.where(first, weights_ref[0:1, :], 0.0) + jnp.where(
                second, weights_ref[1:2, :], 0.0
            )
            factor_ref[...] = jnp.sum(jnp.where(picked, value, 0.0), axis=1, keepdims=True)

        val = jnp.dot(pick_ref[...], source_ref[...], preferred_element_type=F32)
        if scale:
            val = val * factor_ref[...]
        sub = jnp.bitwise_and(iota((main, 128), 0), 7)
        ninth = jnp.zeros((main, 128), F32)
        for j in range(tiles):
            cols = slice(128 * j, 128 * (j + 1))
            out_ref[0, :, 8 * j : 8 * (j + 1), :] = (
                val[:main, cols].reshape(owners, 8, 128).astype(BF16)
            )
            ninth = jnp.where(sub == j, val[main:, cols], ninth)
        out_ref[0, :, 8 * tiles :, :] = ninth.reshape(owners, 8, 128).astype(BF16)

    return pl.pallas_call(
        kernel,
        grid=(blocks,),
        in_specs=[
            pl.BlockSpec((2, rows), lambda i: (0, 0)),
            pl.BlockSpec((2, rows), lambda i: (0, 0)),
            pl.BlockSpec((rows, part), lambda i: (0, i)),
        ],
        out_specs=pl.BlockSpec((1, owners, 9 * tiles, 128), lambda i: (i, 0, 0, 0)),
        out_shape=jax.ShapeDtypeStruct((blocks, owners, 9 * tiles, 128), BF16),
        scratch_shapes=[pltpu.VMEM((2 * main, rows), BF16), pltpu.VMEM((2 * main, 1), F32)],
        compiler_params=pltpu.CompilerParams(vmem_limit_bytes=3 * VMEM_LIMIT),
        cost_estimate=pl.CostEstimate(
            flops=4 * main * rows * width, bytes_accessed=2 * width * (rows + 9 * owners), transcendentals=0
        ),
        name="pack_rows",
    )(routes_t, weights_t, source)


def pack_weights(gate, up, down, owners):
    depth, total = gate.shape
    wide = total // owners
    full = 3 * wide
    half = depth // 2
    many = 8

    def kernel(gate_ref, up_ref, down_ref, out_ref):
        for e in range(many):
            for n, ref in enumerate((gate_ref, up_ref, down_ref)):
                for h in range(2):
                    to = h * full + n * wide
                    out_ref[e, :, to : to + wide] = ref[h * half : (h + 1) * half, e * wide : (e + 1) * wide]

    spec = pl.BlockSpec((depth, many * wide), lambda i: (0, i))
    return pl.pallas_call(
        kernel,
        grid=(owners // many,),
        in_specs=[spec, spec, spec],
        out_specs=pl.BlockSpec((many, half, 2 * full), lambda i: (i, 0, 0)),
        out_shape=jax.ShapeDtypeStruct((owners, half, 2 * full), BF16),
        compiler_params=pltpu.CompilerParams(vmem_limit_bytes=3 * VMEM_LIMIT),
        cost_estimate=pl.CostEstimate(flops=0, bytes_accessed=12 * depth * total, transcendentals=0),
        name="pack_weights",
    )(gate, up, down)


def unpack_weights(received):
    senders, half, double = received.shape
    full = double // 2
    wide = full // 3
    many = 8
    rows = many * 2 * half

    def kernel(received_ref, pair_ref, down_ref):
        for e in range(many):
            for h in range(2):
                to = slice((2 * e + h) * half, (2 * e + h + 1) * half)
                at = h * full
                pair_ref[to, :] = received_ref[e, :, at : at + 2 * wide]
                down_ref[to, :] = received_ref[e, :, at + 2 * wide : at + full]

    return pl.pallas_call(
        kernel,
        grid=(senders // many,),
        in_specs=[pl.BlockSpec((many, half, double), lambda i: (i, 0, 0))],
        out_specs=[
            pl.BlockSpec((rows, 2 * wide), lambda i: (i, 0)),
            pl.BlockSpec((rows, wide), lambda i: (i, 0)),
        ],
        out_shape=[
            jax.ShapeDtypeStruct((senders * 2 * half, 2 * wide), BF16),
            jax.ShapeDtypeStruct((senders * 2 * half, wide), BF16),
        ],
        compiler_params=pltpu.CompilerParams(vmem_limit_bytes=VMEM_LIMIT),
        cost_estimate=pl.CostEstimate(flops=0, bytes_accessed=4 * received.size, transcendentals=0),
        name="unpack_weights",
    )(received)


def unpack_and_multiply(place, received, weight, chips, first, parts):
    senders, height, _ = received.shape
    tiles = height // 9
    depth, columns = weight.shape
    group = senders // (2 * chips)
    main = group * 8
    half = group * 9 // 2

    def kernel(place_ref, received_ref, weight_ref, rows_ref, keep_ref, send_ref, work_ref):
        core = place_ref[1]
        row, col = iota((main, main), 0), iota((main, main), 1)
        turn = one_if(
            (row % group == lax.shift_right_logical(col, 3)) & (row // group == jnp.bitwise_and(col, 7))
        )
        for j in range(tiles):
            work_ref[:main, 128 * j : 128 * (j + 1)] = (
                received_ref[:, 8 * j : 8 * (j + 1), :].astype(F32).reshape(main, 128).astype(BF16)
            )
        last = received_ref[:, 8 * tiles :, :].astype(F32).reshape(main, 128).astype(BF16)
        ninth = jnp.dot(turn, last, preferred_element_type=F32).astype(BF16)
        for j in range(tiles):
            work_ref[main:, 128 * j : 128 * (j + 1)] = ninth[group * j : group * (j + 1)]
        product = jnp.dot(work_ref[...], weight_ref[...], preferred_element_type=F32)
        low, high = product[:half], product[half:]
        keep_ref[0, 0] = jnp.where(core == 0, low, high)
        send_ref[0, 0] = jnp.where(core == 0, high, low)
        rows_ref[0, 0, core] = work_ref[:half]
        rows_ref[0, 0, 1 - core] = work_ref[half:]

    def slot(i, place_ref):
        return (place_ref[0] + chips - i % chips) % chips

    product_spec = pl.BlockSpec((1, 1, half, columns), lambda i, s: (slot(i, s), i // chips, 0, 0))
    product_shape = jax.ShapeDtypeStruct((chips, parts, half, columns), F32)
    return pl.pallas_call(
        kernel,
        grid_spec=pltpu.PrefetchScalarGridSpec(
            num_scalar_prefetch=1,
            grid=(parts * chips,),
            in_specs=[
                pl.BlockSpec((group, height, 128), lambda i, s: (first * chips + i, 0, 0)),
                pl.BlockSpec((depth, columns), lambda i, s: (0, 0)),
            ],
            out_specs=[
                pl.BlockSpec((1, 1, 2, half, depth), lambda i, s: (i // chips, slot(i, s), 0, 0, 0)),
                product_spec,
                product_spec,
            ],
            scratch_shapes=[pltpu.VMEM((2 * half, depth), BF16)],
        ),
        out_shape=[
            jax.ShapeDtypeStruct((parts, chips, 2, half, depth), BF16),
            product_shape,
            product_shape,
        ],
        compiler_params=pltpu.CompilerParams(vmem_limit_bytes=VMEM_LIMIT),
        cost_estimate=pl.CostEstimate(
            flops=4 * parts * chips * half * depth * columns,
            bytes_accessed=parts * chips * half * (8 * depth + 8 * columns) + 2 * depth * columns,
            transcendentals=0,
        ),
        name="unpack_and_multiply",
    )(place, received, weight)


def add_steps(one, two, kind):
    steps, rows, columns = one.shape

    def kernel(one_ref, two_ref, *out_refs):
        for n in range(steps):
            out_refs[n][...] = (one_ref[n] + two_ref[n]).astype(out_refs[n].dtype)

    whole = pl.BlockSpec(memory_space=pltpu.VMEM)
    return pl.pallas_call(
        kernel,
        in_specs=[whole] * 2,
        out_specs=[whole] * steps,
        out_shape=[
            jax.ShapeDtypeStruct((rows, columns), kind if n else F32) for n in range(steps)
        ],
        compiler_params=pltpu.CompilerParams(vmem_limit_bytes=VMEM_LIMIT),
        cost_estimate=pl.CostEstimate(
            flops=one.size, bytes_accessed=12 * one.size, transcendentals=0
        ),
        name="add_steps",
    )(one, two)


def slopes(total, active, slope, part):
    own, others = total[0], total[1:]
    rows, columns = own.shape

    def kernel(own_ref, *refs):
        active_ref, slope_ref, out_ref = refs[len(others) :]
        back = own_ref[...]
        for ref in refs[: len(others)]:
            back = back + ref[...].astype(F32)
        out_ref[:, :columns] = (back * slope_ref[...]).astype(BF16)
        out_ref[:, columns:] = (back * active_ref[...]).astype(BF16)

    whole = pl.BlockSpec((rows, columns), lambda i: (0, 0))
    mine = pl.BlockSpec((rows, columns), lambda i: (part, 0))
    return pl.pallas_call(
        kernel,
        grid=(1,),
        in_specs=[whole] * len(total) + [mine] * 2,
        out_specs=pl.BlockSpec((rows, 2 * columns), lambda i: (0, 0)),
        out_shape=jax.ShapeDtypeStruct((rows, 2 * columns), BF16),
        compiler_params=pltpu.CompilerParams(vmem_limit_bytes=VMEM_LIMIT),
        cost_estimate=pl.CostEstimate(
            flops=6 * own.size, bytes_accessed=24 * own.size, transcendentals=0
        ),
        name="slopes",
    )(own, *others, active, slope)


def follow(values, earlier):
    count = len(values)

    def kernel(*refs):
        del refs

    return pl.pallas_call(
        kernel,
        in_specs=[ANYWHERE] * (count + len(earlier)),
        out_specs=[ANYWHERE] * count,
        out_shape=[jax.ShapeDtypeStruct(v.shape, v.dtype) for v in values],
        input_output_aliases={n: n for n in range(count)},
        name="follow",
    )(*values, *earlier)


def contract_rows(pieces, rows):
    parts, chips, cores, half, depth = rows.shape
    columns = pieces[0].shape[1]
    outs = 1 + columns // 896
    hidden = columns // outs
    count = len(pieces)
    height = parts * count * half
    wide = 256

    def kernel(*refs):
        piece_refs, rows_ref = refs[:count], refs[count]
        out_refs, done_ref = refs[count + 1 : -3], refs[-3]
        left_ref, turned_ref = refs[-2:]
        done_ref[...] = jnp.zeros_like(done_ref)

        @pl.when(pl.program_id(0) == 0)
        def _():
            for p in range(parts):
                for n in range(count):
                    to = (p * count + n) * half
                    left_ref[to : to + half] = piece_refs[n][p * half : (p + 1) * half]
            turned_ref[...] = left_ref[...].T

        right = rows_ref[...].reshape(height, wide)
        product = jnp.dot(turned_ref[...], right, preferred_element_type=F32)
        for n in range(outs):
            out_refs[n][...] = product[n * hidden : (n + 1) * hidden]

    return pl.pallas_call(
        kernel,
        grid=(depth // wide,),
        in_specs=[pl.BlockSpec(piece.shape, lambda i: (0, 0)) for piece in pieces]
        + [pl.BlockSpec(rows.shape[:4] + (wide,), lambda i: (0, 0, 0, 0, i))],
        out_specs=[pl.BlockSpec((hidden, wide), lambda i: (0, i))] * outs
        + [pl.BlockSpec((8, 128), lambda i: (0, 0))],
        out_shape=[jax.ShapeDtypeStruct((hidden, depth), F32)] * outs
        + [jax.ShapeDtypeStruct((8, 128), F32)],
        scratch_shapes=[pltpu.VMEM((height, columns), BF16), pltpu.VMEM((columns, height), BF16)],
        compiler_params=pltpu.CompilerParams(vmem_limit_bytes=3 * VMEM_LIMIT),
        cost_estimate=pl.CostEstimate(
            flops=2 * height * depth * columns,
            bytes_accessed=2 * height * (depth + columns) + 4 * columns * depth,
            transcendentals=0,
        ),
        name="contract_rows",
    )(*pieces, rows)


def flat(value):
    return value.reshape(-1, value.shape[-1])


def per_device(tokens, cotangent, routes, combine_weights, gate_dense, up_dense, down_dense):
    blocks, owners = lax.axis_size("dp"), lax.axis_size("expert")
    chips = blocks // 2
    hidden = gate_dense.shape[1] // owners
    routes_t, weights_t = routes.T, combine_weights.T
    dp = lax.axis_index("dp")
    place = jnp.stack([dp // 2, dp % 2]).astype(jnp.int32)

    def along_x(step, value):
        if step % chips == 0:
            return value
        pairs = [(2 * i + c, 2 * ((i + step) % chips) + c) for i in range(chips) for c in range(2)]
        return lax.ppermute(value, "dp", pairs)

    def other_core(value):
        return lax.ppermute(value, "dp", [(i, i ^ 1) for i in range(blocks)])

    def packed(source, scale):
        return pack_rows(routes_t, weights_t, source, owners, blocks, scale)

    def exchange(send):
        send = send.reshape((-1,) + send.shape[-2:])
        return lax.all_to_all(send, ("dp", "expert"), split_axis=0, concat_axis=0, tiled=True)

    def reduce_rows(keep, send):
        keep, send = (value.reshape(chips, -1, value.shape[-1]) for value in (keep, send))
        sums = add_steps(keep, other_core(send), BF16)
        return [sums[0]] + [along_x(-step, sums[step]) for step in range(1, chips)]

    def gather_rows(value, after=()):
        pieces = []
        for step in range(chips):
            piece = along_x(step, value)
            if after and step == chips - 1:
                (piece,) = follow([piece], after)
            pieces += [piece, other_core(piece)]
        return pieces

    w_send = pack_weights(gate_dense, up_dense, down_dense, owners)
    w_received = lax.all_to_all(w_send, "expert", split_axis=0, concat_axis=0, tiled=True)
    w_pair, w_down = unpack_weights(w_received)

    dy_send = packed(cotangent, True)
    (x_send,) = follow([packed(tokens, False)], [dy_send])
    x_received = exchange(x_send)
    dy_received = exchange(dy_send)

    x_rows, keep, send = unpack_and_multiply(place, x_received, w_pair, chips, 0, 2)
    pair = sum(total.astype(F32) for total in reduce_rows(keep, send))
    gate_vals, up_vals = pair[:, :hidden], pair[:, hidden:]
    sigma = jax.nn.sigmoid(gate_vals)
    active = gate_vals * sigma
    slope = up_vals * (sigma * (1.0 + gate_vals * (1.0 - sigma)))
    hidden_all = gather_rows((active * up_vals).astype(BF16))
    (dy_received,) = follow([dy_received], hidden_all)

    dy_rows, keep, send = unpack_and_multiply(place, dy_received, w_down, chips, 0, 2)
    d_pair = slopes(reduce_rows(keep, send), active, slope, 0)
    grad_down, down_done = contract_rows(hidden_all, dy_rows)
    grad_gate, grad_up, _ = contract_rows(gather_rows(d_pair, [down_done]), x_rows)
    return (grad_gate.T, grad_up.T, grad_down.T)


def solution(mesh):
    split = P(("dp", "expert"), None)
    return jax.shard_map(
        per_device,
        mesh=mesh,
        in_specs=(split,) * 7,
        out_specs=(P("dp", "expert"),) * 3,
        check_vma=False,
    )
```

```python
import jax
import jax.numpy as jnp
from jax import lax
from jax.experimental import pallas as pl
from jax.experimental.pallas import tpu as pltpu
from jax.sharding import PartitionSpec as P

F32 = jnp.float32
BF16 = jnp.bfloat16
VMEM_LIMIT = 20 * 1024 * 1024
ANYWHERE = pl.BlockSpec(memory_space=pl.ANY)


def iota(shape, dim):
    return lax.broadcasted_iota(jnp.int32, shape, dim)


def one_if(mask):
    return jnp.where(mask, 1.0, 0.0).astype(BF16)


def pack_rows(routes_t, weights_t, source, owners, blocks, scale):
    rows, width = source.shape
    part = width // blocks
    tiles = part // 128
    main = owners * 8

    def kernel(routes_ref, weights_ref, source_ref, out_ref, pick_ref, factor_ref):
        @pl.when(pl.program_id(0) == 0)
        def _():
            row = iota((2 * main, rows), 0)
            expert = lax.shift_right_logical(jnp.where(row < main, row, row - main), 3)
            first = routes_ref[0:1, :] == expert
            second = routes_ref[1:2, :] == expert
            named = first | second
            before = one_if(iota((rows, rows), 0) < iota((rows, rows), 1))
            rank = jnp.dot(one_if(named), before, preferred_element_type=F32)
            wanted = jnp.where(row < main, jnp.bitwise_and(row, 7), 8).astype(F32)
            picked = named & (rank == wanted)
            pick_ref[...] = one_if(picked)
            value = jnp.where(first, weights_ref[0:1, :], 0.0) + jnp.where(
                second, weights_ref[1:2, :], 0.0
            )
            factor_ref[...] = jnp.sum(jnp.where(picked, value, 0.0), axis=1, keepdims=True)

        val = jnp.dot(pick_ref[...], source_ref[...], preferred_element_type=F32)
        if scale:
            val = val * factor_ref[...]
        sub = jnp.bitwise_and(iota((main, 128), 0), 7)
        ninth = jnp.zeros((main, 128), F32)
        for j in range(tiles):
            cols = slice(128 * j, 128 * (j + 1))
            out_ref[0, :, 8 * j : 8 * (j + 1), :] = (
                val[:main, cols].reshape(owners, 8, 128).astype(BF16)
            )
            ninth = jnp.where(sub == j, val[main:, cols], ninth)
        out_ref[0, :, 8 * tiles :, :] = ninth.reshape(owners, 8, 128).astype(BF16)

    return pl.pallas_call(
        kernel,
        grid=(blocks,),
        in_specs=[
            pl.BlockSpec((2, rows), lambda i: (0, 0)),
            pl.BlockSpec((2, rows), lambda i: (0, 0)),
            pl.BlockSpec((rows, part), lambda i: (0, i)),
        ],
        out_specs=pl.BlockSpec((1, owners, 9 * tiles, 128), lambda i: (i, 0, 0, 0)),
        out_shape=jax.ShapeDtypeStruct((blocks, owners, 9 * tiles, 128), BF16),
        scratch_shapes=[pltpu.VMEM((2 * main, rows), BF16), pltpu.VMEM((2 * main, 1), F32)],
        compiler_params=pltpu.CompilerParams(vmem_limit_bytes=3 * VMEM_LIMIT),
        cost_estimate=pl.CostEstimate(
            flops=4 * main * rows * width, bytes_accessed=2 * width * (rows + 9 * owners), transcendentals=0
        ),
        name="pack_rows",
    )(routes_t, weights_t, source)


def pack_weights(gate, up, down, owners):
    depth, total = gate.shape
    wide = total // owners
    full = 3 * wide
    half = depth // 2
    many = 8

    def kernel(gate_ref, up_ref, down_ref, out_ref):
        for e in range(many):
            for n, ref in enumerate((gate_ref, up_ref, down_ref)):
                for h in range(2):
                    to = h * full + n * wide
                    out_ref[e, :, to : to + wide] = ref[h * half : (h + 1) * half, e * wide : (e + 1) * wide]

    spec = pl.BlockSpec((depth, many * wide), lambda i: (0, i))
    return pl.pallas_call(
        kernel,
        grid=(owners // many,),
        in_specs=[spec, spec, spec],
        out_specs=pl.BlockSpec((many, half, 2 * full), lambda i: (i, 0, 0)),
        out_shape=jax.ShapeDtypeStruct((owners, half, 2 * full), BF16),
        compiler_params=pltpu.CompilerParams(vmem_limit_bytes=3 * VMEM_LIMIT),
        cost_estimate=pl.CostEstimate(flops=0, bytes_accessed=12 * depth * total, transcendentals=0),
        name="pack_weights",
    )(gate, up, down)


def unpack_weights(received):
    senders, half, double = received.shape
    full = double // 2
    wide = full // 3
    many = 8
    rows = many * 2 * half

    def kernel(received_ref, pair_ref, down_ref):
        for e in range(many):
            for h in range(2):
                to = slice((2 * e + h) * half, (2 * e + h + 1) * half)
                at = h * full
                pair_ref[to, :] = received_ref[e, :, at : at + 2 * wide]
                down_ref[to, :] = received_ref[e, :, at + 2 * wide : at + full]

    return pl.pallas_call(
        kernel,
        grid=(senders // many,),
        in_specs=[pl.BlockSpec((many, half, double), lambda i: (i, 0, 0))],
        out_specs=[
            pl.BlockSpec((rows, 2 * wide), lambda i: (i, 0)),
            pl.BlockSpec((rows, wide), lambda i: (i, 0)),
        ],
        out_shape=[
            jax.ShapeDtypeStruct((senders * 2 * half, 2 * wide), BF16),
            jax.ShapeDtypeStruct((senders * 2 * half, wide), BF16),
        ],
        compiler_params=pltpu.CompilerParams(vmem_limit_bytes=VMEM_LIMIT),
        cost_estimate=pl.CostEstimate(flops=0, bytes_accessed=4 * received.size, transcendentals=0),
        name="unpack_weights",
    )(received)


def unpack_and_multiply(place, received, weight, chips, first, parts):
    senders, height, _ = received.shape
    tiles = height // 9
    depth, columns = weight.shape
    group = senders // (2 * chips)
    main = group * 8
    half = group * 9 // 2

    def kernel(place_ref, received_ref, weight_ref, rows_ref, keep_ref, send_ref, work_ref):
        core = place_ref[1]
        row, col = iota((main, main), 0), iota((main, main), 1)
        turn = one_if(
            (row % group == lax.shift_right_logical(col, 3)) & (row // group == jnp.bitwise_and(col, 7))
        )
        for j in range(tiles):
            work_ref[:main, 128 * j : 128 * (j + 1)] = (
                received_ref[:, 8 * j : 8 * (j + 1), :].astype(F32).reshape(main, 128).astype(BF16)
            )
        last = received_ref[:, 8 * tiles :, :].astype(F32).reshape(main, 128).astype(BF16)
        ninth = jnp.dot(turn, last, preferred_element_type=F32).astype(BF16)
        for j in range(tiles):
            work_ref[main:, 128 * j : 128 * (j + 1)] = ninth[group * j : group * (j + 1)]
        product = jnp.dot(work_ref[...], weight_ref[...], preferred_element_type=F32)
        low, high = product[:half], product[half:]
        keep_ref[0, 0] = jnp.where(core == 0, low, high)
        send_ref[0, 0] = jnp.where(core == 0, high, low)
        rows_ref[0, 0, core] = work_ref[:half]
        rows_ref[0, 0, 1 - core] = work_ref[half:]

    def slot(i, place_ref):
        return (place_ref[0] + chips - i % chips) % chips

    product_spec = pl.BlockSpec((1, 1, half, columns), lambda i, s: (slot(i, s), i // chips, 0, 0))
    product_shape = jax.ShapeDtypeStruct((chips, parts, half, columns), F32)
    return pl.pallas_call(
        kernel,
        grid_spec=pltpu.PrefetchScalarGridSpec(
            num_scalar_prefetch=1,
            grid=(parts * chips,),
            in_specs=[
                pl.BlockSpec((group, height, 128), lambda i, s: (first * chips + i, 0, 0)),
                pl.BlockSpec((depth, columns), lambda i, s: (0, 0)),
            ],
            out_specs=[
                pl.BlockSpec((1, 1, 2, half, depth), lambda i, s: (i // chips, slot(i, s), 0, 0, 0)),
                product_spec,
                product_spec,
            ],
            scratch_shapes=[pltpu.VMEM((2 * half, depth), BF16)],
        ),
        out_shape=[
            jax.ShapeDtypeStruct((parts, chips, 2, half, depth), BF16),
            product_shape,
            product_shape,
        ],
        compiler_params=pltpu.CompilerParams(vmem_limit_bytes=VMEM_LIMIT),
        cost_estimate=pl.CostEstimate(
            flops=4 * parts * chips * half * depth * columns,
            bytes_accessed=parts * chips * half * (8 * depth + 8 * columns) + 2 * depth * columns,
            transcendentals=0,
        ),
        name="unpack_and_multiply",
    )(place, received, weight)


def add_steps(one, two, kind):
    steps, rows, columns = one.shape
    folded = columns % 128 > 0
    sent = (rows // 2, 2 * columns) if folded else (rows, columns)

    def kernel(one_ref, two_ref, *out_refs):
        for n in range(steps):
            total = (one_ref[n] + two_ref[n]).astype(out_refs[n].dtype)
            if n and folded:
                out_refs[n][:, :columns] = total[: rows // 2]
                out_refs[n][:, columns:] = total[rows // 2 :]
            else:
                out_refs[n][...] = total

    whole = pl.BlockSpec(memory_space=pltpu.VMEM)
    return pl.pallas_call(
        kernel,
        in_specs=[whole] * 2,
        out_specs=[whole] * steps,
        out_shape=[
            jax.ShapeDtypeStruct(sent, kind) if n else jax.ShapeDtypeStruct((rows, columns), F32)
            for n in range(steps)
        ],
        compiler_params=pltpu.CompilerParams(vmem_limit_bytes=VMEM_LIMIT),
        cost_estimate=pl.CostEstimate(
            flops=one.size, bytes_accessed=12 * one.size, transcendentals=0
        ),
        name="add_steps",
    )(one, two)


def slopes(total, active, slope):
    own, others = total[0], total[1:]
    rows, columns = own.shape
    half = rows // 2

    def kernel(own_ref, *refs):
        active_ref, slope_ref, out_ref = refs[len(others) :]
        for h in range(2):
            mine = slice(h * half, (h + 1) * half)
            back = own_ref[mine]
            for ref in refs[: len(others)]:
                back = back + ref[:, h * columns : (h + 1) * columns].astype(F32)
            out_ref[mine, :columns] = (back * slope_ref[mine]).astype(BF16)
            out_ref[mine, columns:] = (back * active_ref[mine]).astype(BF16)

    whole = pl.BlockSpec(memory_space=pltpu.VMEM)
    return pl.pallas_call(
        kernel,
        in_specs=[whole] * (len(total) + 2),
        out_specs=whole,
        out_shape=jax.ShapeDtypeStruct((rows, 2 * columns), BF16),
        compiler_params=pltpu.CompilerParams(vmem_limit_bytes=VMEM_LIMIT),
        cost_estimate=pl.CostEstimate(
            flops=6 * own.size, bytes_accessed=24 * own.size, transcendentals=0
        ),
        name="slopes",
    )(own, *others, active, slope)


def follow(values, earlier):
    count = len(values)

    def kernel(*refs):
        del refs

    return pl.pallas_call(
        kernel,
        in_specs=[ANYWHERE] * (count + len(earlier)),
        out_specs=[ANYWHERE] * count,
        out_shape=[jax.ShapeDtypeStruct(v.shape, v.dtype) for v in values],
        input_output_aliases={n: n for n in range(count)},
        name="follow",
    )(*values, *earlier)


def contract_rows(pieces, rows):
    parts, chips, cores, half, depth = rows.shape
    columns = pieces[0].shape[1]
    outs = 1 + columns // 896
    hidden = columns // outs
    count = len(pieces)
    height = parts * count * half
    wide = 256

    def kernel(*refs):
        piece_refs, rows_ref = refs[:count], refs[count]
        out_refs, done_ref = refs[count + 1 : -2], refs[-2]
        left_ref = refs[-1]
        done_ref[...] = jnp.zeros_like(done_ref)

        @pl.when(pl.program_id(0) == 0)
        def _():
            for p in range(parts):
                for n in range(count):
                    to = (p * count + n) * half
                    left_ref[to : to + half] = piece_refs[n][p * half : (p + 1) * half]

        right = rows_ref[...].reshape(height, wide)
        product = lax.dot_general(
            left_ref[...], right, (((0,), (0,)), ((), ())), preferred_element_type=F32
        )
        for n in range(outs):
            out_refs[n][...] = product[n * hidden : (n + 1) * hidden]

    return pl.pallas_call(
        kernel,
        grid=(depth // wide,),
        in_specs=[pl.BlockSpec(piece.shape, lambda i: (0, 0)) for piece in pieces]
        + [pl.BlockSpec(rows.shape[:4] + (wide,), lambda i: (0, 0, 0, 0, i))],
        out_specs=[pl.BlockSpec((hidden, wide), lambda i: (0, i))] * outs
        + [pl.BlockSpec((8, 128), lambda i: (0, 0))],
        out_shape=[jax.ShapeDtypeStruct((hidden, depth), F32)] * outs
        + [jax.ShapeDtypeStruct((8, 128), F32)],
        scratch_shapes=[pltpu.VMEM((height, columns), BF16)],
        compiler_params=pltpu.CompilerParams(vmem_limit_bytes=3 * VMEM_LIMIT),
        cost_estimate=pl.CostEstimate(
            flops=2 * height * depth * columns,
            bytes_accessed=2 * height * (depth + columns) + 4 * columns * depth,
            transcendentals=0,
        ),
        name="contract_rows",
    )(*pieces, rows)


def flat(value):
    return value.reshape(-1, value.shape[-1])


def per_device(tokens, cotangent, routes, combine_weights, gate_dense, up_dense, down_dense):
    blocks, owners = lax.axis_size("dp"), lax.axis_size("expert")
    chips = blocks // 2
    hidden = gate_dense.shape[1] // owners
    routes_t, weights_t = routes.T, combine_weights.T
    dp = lax.axis_index("dp")
    place = jnp.stack([dp // 2, dp % 2]).astype(jnp.int32)

    def along_x(step, value):
        if step % chips == 0:
            return value
        pairs = [(2 * i + c, 2 * ((i + step) % chips) + c) for i in range(chips) for c in range(2)]
        return lax.ppermute(value, "dp", pairs)

    def other_core(value):
        return lax.ppermute(value, "dp", [(i, i ^ 1) for i in range(blocks)])

    def packed(source, scale):
        return pack_rows(routes_t, weights_t, source, owners, blocks, scale)

    def exchange(send):
        send = send.reshape((-1,) + send.shape[-2:])
        return lax.all_to_all(send, ("dp", "expert"), split_axis=0, concat_axis=0, tiled=True)

    def reduce_rows(keep, send):
        keep, send = (value.reshape(chips, -1, value.shape[-1]) for value in (keep, send))
        sums = add_steps(keep, other_core(send), BF16)
        return [sums[0]] + [along_x(-step, sums[step]) for step in range(1, chips)]

    def gather_rows(value, after=()):
        pieces = []
        for step in range(chips):
            piece = along_x(step, value)
            if after and step == chips - 1:
                (piece,) = follow([piece], after)
            pieces += [piece, other_core(piece)]
        return pieces

    w_send = pack_weights(gate_dense, up_dense, down_dense, owners)
    w_received = lax.all_to_all(w_send, "expert", split_axis=0, concat_axis=0, tiled=True)
    w_pair, w_down = unpack_weights(w_received)

    dy_send = packed(cotangent, True)
    (x_send,) = follow([packed(tokens, False)], [dy_send])
    x_received = exchange(x_send)
    dy_received = exchange(dy_send)

    x_rows, keep, send = unpack_and_multiply(place, x_received, w_pair, chips, 0, 2)
    pair = sum(total.astype(F32) for total in reduce_rows(keep, send))
    gate_vals, up_vals = pair[:, :hidden], pair[:, hidden:]
    sigma = jax.nn.sigmoid(gate_vals)
    active = gate_vals * sigma
    slope = up_vals * (sigma * (1.0 + gate_vals * (1.0 - sigma)))
    hidden_all = gather_rows((active * up_vals).astype(BF16))
    (dy_received,) = follow([dy_received], hidden_all)

    dy_rows, keep, send = unpack_and_multiply(place, dy_received, w_down, chips, 0, 2)
    d_pair = slopes(reduce_rows(keep, send), active, slope)
    grad_down, down_done = contract_rows(hidden_all, dy_rows)
    grad_gate, grad_up, _ = contract_rows(gather_rows(d_pair, [down_done]), x_rows)
    return (grad_gate.T, grad_up.T, grad_down.T)


def solution(mesh):
    split = P(("dp", "expert"), None)
    return jax.shard_map(
        per_device,
        mesh=mesh,
        in_specs=(split,) * 7,
        out_specs=(P("dp", "expert"),) * 3,
        check_vma=False,
    )
```
